256 devices in a mesh: frame: 32 (over y_lo, z, core), space: 8 (over x, y_hi).
Axes of the slice: x: 4, y: 4 (y_hi: 2, y_lo: 2; y = y_hi * 2 + y_lo), z: 8, core: 2. Of those that a mesh axis runs over, the one named last changes fastest.
Arguments:
- latents: float32 [64, 16, 1024], P('frame', None, 'space'), may hold values from -6 to 6
- time_index: int32 [64], P('frame'), may hold values from 0 to 127, as said below
- fresh_noise: float32 [16, 1024], P(None, 'space'), may hold values from -6 to 6
- modulation_table: bfloat16 [128, 8, 1152], replicated, may hold values from -3 to 3
- embed_weight: bfloat16 [16, 1152], replicated, may hold values from -1.5 to 1.5
- spatial_qkv: bfloat16 [1152, 3456], P(None, 'space'), may hold values from -0.1875 to 0.1875
- spatial_out: bfloat16 [1152, 1152], P('space'), may hold values from -0.1875 to 0.1875
- temporal_qkv: bfloat16 [1152, 3456], P(None, 'space'), may hold values from -0.1875 to 0.1875
- temporal_out: bfloat16 [1152, 1152], P('space'), may hold values from -0.1875 to 0.1875
- final_weight: bfloat16 [1152, 16], replicated, may hold values from -0.1875 to 0.1875
- spatial_gain: float32 [2, 72], replicated, may hold values from 1 to 2.5
- temporal_gain: float32 [2, 72], replicated, may hold values from 1 to 2.5
Outputs:
- velocity: float32 [64, 16, 1024], P('frame', None, 'space')
- queue_next: float32 [64, 16, 1024], P('frame', None, 'space')
The draws below stay inside these ranges and needn't reach their ends.
Inputs may be any that keep to these rules, and one draw needn't show every extreme that they name: `time_index`: 64 distinct indices rising along the queue; the first is 0 and the last is 127.
All inputs are finite; a program needn't handle non-finite values.
Results may differ from the reference program's by a relative error of at most 0.02.
Values may be sent and summed in bfloat16 or wider, within the bound.
A program may use at most 128 MiB of HBM per device.

```python
import math
import jax
import jax.numpy as jnp
from jax import lax

D = 1152
HEADS = 16
HEAD_DIM = 72
PATCH = 16
S_DEV = 128
FRAMES = 64
TOK_FRAME = 1024
STEPS = 128


def draw_time_index(key, part):
    key = jax.random.fold_in(key, 11)
    inner = jax.random.permutation(key, STEPS - 2) + 1
    chosen = jnp.sort(inner[:FRAMES - 2]).astype(jnp.int32)
    first = jnp.zeros((1,), jnp.int32)
    final = jnp.full((1,), STEPS - 1, jnp.int32)
    return jnp.concatenate([first, chosen, final])


def steps_of(own_key, extent, split, least, largest):
    level, own = 1.0, jax.random.fold_in(own_key, 6)
    for axis_at, parts in split:
        steps = jnp.exp(jax.random.uniform(jax.random.fold_in(own, axis_at), (parts,), jnp.float32, least / len(split), largest / len(split)))
        level = level * jnp.repeat(steps, extent[axis_at] // parts).reshape([-1 if axis == axis_at else 1 for axis in range(len(extent))])
    return level


def scatter_about(own_key, extent, scale, most, shards=(), kind=jnp.bfloat16):
    values = jax.random.normal(own_key, extent, jnp.float32) * scale
    if len(shards) > 0:
        values = steps_of(own_key, extent, shards, -0.22, 0.18) * values
    return jnp.clip(values, min=-most, max=most).astype(kind)


def setup_inputs(seed: int = 0) -> dict:
    key_of = jax.random.split(jax.random.key(seed), 13)
    return {
        "latents": scatter_about(key_of[0], (FRAMES, PATCH, TOK_FRAME), 1.0, 6.0, ((0, 32), (2, 8)), jnp.float32),
        "time_index": draw_time_index(jax.random.fold_in(key_of[12], 71), 0),
        "fresh_noise": scatter_about(key_of[2], (PATCH, TOK_FRAME), 1.0, 6.0, ((1, 8),), jnp.float32),
        "modulation_table": scatter_about(key_of[3], (STEPS, 8, D), 0.5, 3.0),
        "embed_weight": scatter_about(key_of[4], (PATCH, D), PATCH ** -0.5, 1.5),
        "spatial_qkv": scatter_about(key_of[5], (D, 3 * D), D ** -0.5, 0.1875, ((1, 8),)),
        "spatial_out": scatter_about(key_of[6], (D, D), D ** -0.5, 0.1875, ((0, 8),)),
        "temporal_qkv": scatter_about(key_of[7], (D, 3 * D), D ** -0.5, 0.1875, ((1, 8),)),
        "temporal_out": scatter_about(key_of[8], (D, D), D ** -0.5, 0.1875, ((0, 8),)),
        "final_weight": scatter_about(key_of[9], (D, PATCH), D ** -0.5, 0.1875),
        "spatial_gain": jnp.clip(jnp.exp(jax.random.uniform(key_of[10], (2, HEAD_DIM), jnp.float32, math.log(1.0), math.log(2.5))), 1.0, 2.5),
        "temporal_gain": jnp.clip(jnp.exp(jax.random.uniform(key_of[11], (2, HEAD_DIM), jnp.float32, math.log(1.0), math.log(2.5))), 1.0, 2.5),
    }


time_shift = 3.0
norm_eps = 1e-06

def level(index, total):
    fraction = index.astype(jnp.float32) / total
    return time_shift * fraction / (1.0 + (time_shift - 1.0) * fraction)

def layer_norm(values):
    center = values - lax.optimization_barrier(jnp.mean(values, axis=-1, keepdims=True))
    spread = lax.optimization_barrier(jnp.mean(center * center, axis=-1, keepdims=True))
    return center / jnp.sqrt(spread + norm_eps)

def head_norm(values, gain):
    power = lax.optimization_barrier(jnp.mean(values * values, axis=-1, keepdims=True))
    return values / jnp.sqrt(power + norm_eps) * gain

def split_heads(projected, gain):
    query = head_norm(projected[..., 0, :], gain[0]).astype(jnp.bfloat16)
    keys = head_norm(projected[..., 1, :], gain[1]).astype(jnp.bfloat16)
    values = projected[..., 2, :].astype(jnp.bfloat16)
    return (query, keys, values)

def spatial_frame(state, modulation, spatial_qkv, spatial_out, spatial_gain):
    tokens = state.shape[0]
    ready = (layer_norm(state) * (1.0 + modulation[1]) + modulation[0]).astype(jnp.bfloat16)
    projected = jnp.dot(ready, spatial_qkv, preferred_element_type=jnp.float32).reshape(tokens, HEADS, 3, HEAD_DIM)
    query, keys, values = split_heads(projected, spatial_gain)
    score_scale = HEAD_DIM ** (-0.5)
    scores = jnp.einsum('qhc,khc->hqk', query.astype(jnp.float32), keys.astype(jnp.float32)) * score_scale
    weights = jnp.exp(scores)
    total = lax.optimization_barrier(jnp.sum(weights, axis=-1))
    rounded = lax.optimization_barrier(weights.astype(jnp.bfloat16))
    weighted = jnp.einsum('hqk,khc->qhc', rounded.astype(jnp.float32), values.astype(jnp.float32))
    attended = (weighted / jnp.transpose(total)[:, :, None]).astype(jnp.bfloat16).reshape(tokens, HEADS * HEAD_DIM)
    output = jnp.dot(attended, spatial_out, preferred_element_type=jnp.float32)
    return state + modulation[2] * output

def temporal_group(state, modulation, temporal_qkv, temporal_out, temporal_gain):
    frames, group = (state.shape[0], state.shape[1])
    ready = (layer_norm(state) * (1.0 + modulation[:, None, 4]) + modulation[:, None, 3]).astype(jnp.bfloat16)
    projected = jnp.dot(ready.reshape(frames * group, D), temporal_qkv, preferred_element_type=jnp.float32)
    projected = projected.reshape(frames, group, HEADS, 3, HEAD_DIM)
    query, keys, values = split_heads(projected, temporal_gain)
    score_scale = HEAD_DIM ** (-0.5)
    scores = jnp.einsum('fghc,kghc->ghfk', query.astype(jnp.float32), keys.astype(jnp.float32)) * score_scale
    weights = jnp.exp(scores)
    total = lax.optimization_barrier(jnp.sum(weights, axis=-1))
    rounded = lax.optimization_barrier(weights.astype(jnp.bfloat16))
    weighted = jnp.einsum('ghfk,kghc->fghc', rounded.astype(jnp.float32), values.astype(jnp.float32))
    attended = (weighted / jnp.transpose(total, (2, 0, 1))[..., None]).astype(jnp.bfloat16)
    output = jnp.dot(attended.reshape(frames * group, D), temporal_out, preferred_element_type=jnp.float32)
    return state + modulation[:, None, 5] * output.reshape(frames, group, D)

def reference(latents, time_index, fresh_noise, modulation_table, embed_weight, spatial_qkv, spatial_out, temporal_qkv, temporal_out, final_weight, spatial_gain, temporal_gain):
    modulation = modulation_table[time_index].astype(jnp.float32)
    tokens_in = latents.astype(jnp.bfloat16).astype(jnp.float32)
    hidden = jnp.einsum('fct,cd->ftd', tokens_in, embed_weight.astype(jnp.float32))

    def one_frame(pair):
        return spatial_frame(pair[0], pair[1], spatial_qkv, spatial_out, spatial_gain)
    hidden = lax.map(one_frame, (hidden, modulation))
    groups = TOK_FRAME // S_DEV
    grouped = jnp.transpose(hidden.reshape(FRAMES, groups, S_DEV, D), (1, 0, 2, 3))

    def one_group(block):
        return temporal_group(block, modulation, temporal_qkv, temporal_out, temporal_gain)
    grouped = lax.map(one_group, grouped)
    hidden = jnp.transpose(grouped, (1, 0, 2, 3)).reshape(FRAMES, TOK_FRAME, D)
    ready = (layer_norm(hidden) * (1.0 + modulation[:, None, 7]) + modulation[:, None, 6]).astype(jnp.bfloat16)
    predicted = jnp.dot(ready.reshape(FRAMES * TOK_FRAME, D), final_weight, preferred_element_type=jnp.float32)
    velocity = jnp.transpose(predicted.reshape(FRAMES, TOK_FRAME, PATCH), (0, 2, 1))
    step_size = level(time_index + 1, STEPS) - level(time_index, STEPS)
    updated = latents - step_size[:, None, None] * velocity
    queue_next = jnp.concatenate([updated[1:], fresh_noise[None]], axis=0)
    return (velocity, queue_next)
```

```python
import jax
import jax.numpy as jnp
from jax import lax
from jax.experimental import pallas as pl
from jax.experimental.pallas import tpu as pltpu
from jax.sharding import PartitionSpec as P

HD = 72
D = 1152
NF = 32
NS = 8
STEPS = 128
PATCH = 16
TOK = 1024
OWN = 128
SUB = 4
SHARD = 768
QUARTER = SHARD // 4
OUT_S, QKV_T, OUT_T = 0, 144, 576
ROWS = 2 * SUB * NF
WIDE = 640
EPS = 1e-6
LOG2E = 1.4426950408889634
SCORE = HD ** -0.5 * LOG2E
BF = jnp.bfloat16
F32 = jnp.float32

NN = (((1,), (0,)), ((), ()))
NT = (((1,), (1,)), ((), ()))


def dot(a, b, dims=NN, precision=None):
    return lax.dot_general(a, b, dims, preferred_element_type=F32, precision=precision)


def iota(shape, axis):
    return lax.broadcasted_iota(jnp.int32, shape, axis)


def split2(a):
    high = a.astype(BF)
    return high, (a - high.astype(F32)).astype(BF)


def split3(a):
    high = a.astype(BF)
    rest = a - high.astype(F32)
    mid = rest.astype(BF)
    return high, mid, (rest - mid.astype(F32)).astype(BF)


def layer_norm(a):
    center = a - jnp.mean(a, axis=-1, keepdims=True)
    spread = jnp.mean(center * center, axis=-1, keepdims=True)
    return center * lax.rsqrt(spread + EPS)


def head_norm(a, gain):
    return a * lax.rsqrt(jnp.mean(a * a, axis=0, keepdims=True) + EPS) * gain


def level(index):
    fraction = index * (1.0 / STEPS)
    return 3.0 * fraction / (1.0 + 2.0 * fraction)


def kernel(
    latents, steps, noise, table, embed, qkv_s, out_s, qkv_t, out_t, final, gains,
    velocity, queue,
    weights, lat_send, lat_all, lat_next, step_rows, qb, kb, vb, att_f, att, att_in, send, recv,
    mods, proj, att_t, vel_send, vel_recv,
    lat_ssem, lat_rsem, next_sem, step_ssem, step_rsem, dir_ssem, dir_rsem, core_ssem, core_rsem,
    att_ssem, att_rsem, row_ssem, row_rsem, vel_ssem, vel_rsem, own_sem,
):
    f = lax.axis_index("frame")
    s = lax.axis_index("space")
    c = f % 2
    yl = f // 16
    x = s // 2
    yh = s % 2

    def frame_peer(k):
        return lax.rem(f + k, NF)

    def space_peer(k):
        return lax.rem(s + k, NS)

    step = 1 - 2 * c
    to_x = (f, lax.rem(x + step + 4, 4) * 2 + yh)
    to_core = (f + step, s)
    to_cross = (lax.rem(f + 16, NF), 2 * x + 1 - yh)
    to_side = (lax.rem(f + 16, NF), s)

    barrier = pltpu.get_barrier_semaphore()

    def greet(target):
        pl.semaphore_signal(barrier, inc=1, device_id=target, device_id_type=pl.DeviceIdType.MESH)

    @pl.loop(1, NF)
    def _(k):
        greet((frame_peer(k), s))

    @pl.loop(1, NS)
    def _(k):
        greet((f, space_peer(k)))

    greet(to_cross)

    def push(src, dst, ssem, rsem, target):
        return pltpu.make_async_remote_copy(
            src_ref=src, dst_ref=dst, send_sem=ssem, recv_sem=rsem,
            device_id=target, device_id_type=pl.DeviceIdType.MESH,
        )

    for j in range(2):
        lat_send[j] = latents[j].astype(BF)
    weights[s, OUT_S:QKV_T, :] = out_s[...]
    weights[s, OUT_T : OUT_T + 144, :] = out_t[...]
    weights[s, OUT_T + 144 :, :] = jnp.zeros((SHARD - OUT_T - 144, D), BF)
    eye = (iota((432, 432), 0) == iota((432, 432), 1)).astype(BF)
    weights[s, QKV_T:OUT_T, :] = dot(eye, qkv_t[...], NT).astype(BF)
    half = iota((8, 128), 0) < SUB
    own_steps = jnp.where(half, steps[0], steps[1]).astype(F32)
    step_rows[pl.ds(pl.multiple_of(f * 8, 8), 8), :] = own_steps
    step_rows[ROWS:, :] = jnp.zeros((8, 128), F32)
    vel_send[...] = jnp.zeros(vel_send.shape, F32)

    pl.semaphore_wait(barrier, NF + NS - 1)

    def lat_copy(k):
        return push(lat_send, lat_all.at[s], lat_ssem.at[k], lat_rsem.at[s], (f, space_peer(k)))

    def lat_wait(k):
        origin = space_peer(k)
        push(lat_send, lat_all.at[origin], lat_ssem.at[k], lat_rsem.at[origin], (f, origin)).wait_recv()

    def next_copy():
        return push(latents.at[0], lat_next, next_sem.at[0], next_sem.at[1], (frame_peer(NF - 1), s))

    def step_copy(k, row):
        rows = pl.ds(pl.multiple_of(row * 8, 8), 8)
        return push(
            step_rows.at[rows], step_rows.at[rows], step_ssem.at[k], step_rsem.at[row], (frame_peer(k), s)
        )

    @pl.loop(1, NS)
    def _(k):
        lat_copy(k).start()

    own_lat = pltpu.make_async_copy(lat_send, lat_all.at[s], own_sem.at[0])
    own_lat.start()

    def block(i, who):
        turn = 1 - 2 * who
        before = lax.rem(x - turn + 4, 4)
        after = lax.rem(x + turn + 4, 4)
        far = lax.rem(x + 2, 4)
        q = 2 * yl + who
        r = 2 * (1 - yl) + who
        if i < 4:
            return before * 2 + yh, (q, 2 * yl + 1 - who, r, 2 * (1 - yl) + 1 - who)[i]
        if i < 6:
            return far * 2 + yh, (q, r)[i - 4]
        across = (x, before, after, far)[(i - 6) % 4] * 2 + 1 - yh
        return across, (r if i < 10 else q)

    def place(share, quarter):
        return weights.at[share, pl.ds(pl.multiple_of(quarter * QUARTER, QUARTER), QUARTER), :]

    def hop(i, share, quarter):
        target = to_x if i < 6 else to_cross if i < 10 else to_side
        spot = place(share, quarter)
        return push(spot, spot, dir_ssem.at[i], dir_rsem.at[i], target)

    def hop_source(i):
        q = 2 * yl + c
        r = 2 * (1 - yl) + c
        if i < 4:
            return s, (q, 2 * yl + 1 - c, r, 2 * (1 - yl) + 1 - c)[i]
        if i < 6:
            return block((0, 2)[i - 4], c)
        if i < 10:
            near = (x, lax.rem(x - step + 4, 4), lax.rem(x + step + 4, 4), lax.rem(x + 2, 4))[i - 6]
            return near * 2 + yh, q
        return block(i - 4, c)

    def hop_start(i):
        hop(i, *hop_source(i)).start()

    def core_copy(i, who):
        spot = place(*block(i, who))
        return push(spot, spot, core_ssem.at[i], core_rsem.at[i], to_core)

    def take(i, *then):
        hop(i, *block(i, c)).wait_recv()
        core_copy(i, c).start()
        for j in then:
            hop_start(j)

    def take_core(i, *then):
        core_copy(i, 1 - c).wait_recv()
        for j in then:
            hop_start(j)

    hop_start(0)
    hop_start(6)
    hop_start(1)

    @pl.loop(1, NF)
    def _(k):
        step_copy(k, f).start()

    next_copy().start()
    hop_start(2)
    hop_start(3)

    base = embed[...].astype(F32)
    center = base - jnp.mean(base, axis=1, keepdims=True)
    gram = dot(center, center, NT, lax.Precision.HIGHEST) * (1.0 / D)
    gram3 = jnp.concatenate(split3(gram), axis=1)
    pick_row = iota((8, 8 * STEPS), 0)
    pick = jnp.zeros((8, 8 * STEPS), jnp.bool_)
    for j in range(2):
        for kind in range(2):
            pick |= (pick_row == 2 * j + kind) & (iota((8, 8 * STEPS), 1) == steps[j] * 8 + kind)
    own_mods = dot(pick.astype(BF), table[...])
    parts = []
    for j in range(2):
        parts.extend(split2(center * (1.0 + own_mods[2 * j + 1 : 2 * j + 2, :])))
    parts.extend(split2(own_mods))
    stack = jnp.concatenate(parts, axis=0)
    qkv_s_t = dot(eye, qkv_s[...], NT).astype(BF)
    mixed = dot(qkv_s_t, stack, NT)

    own_lat.wait()

    @pl.loop(1, NS)
    def _(k):
        lat_wait(k)

    def project_frame(j):
        lat = jnp.concatenate([lat_all[i, j] for i in range(NS)], axis=1)
        lat32 = lat.astype(F32)
        spread = jnp.sum(lat32 * dot(gram3, jnp.concatenate([lat] * 3, axis=0)), axis=0, keepdims=True)
        rstd = lax.rsqrt(jnp.maximum(spread, 0.0) + EPS)
        matrix = mixed[:, 32 * j : 32 * j + 16] + mixed[:, 32 * j + 16 : 32 * j + 32]
        shift = mixed[:, 64 + 2 * j : 65 + 2 * j] + mixed[:, 72 + 2 * j : 73 + 2 * j]
        matrix2 = jnp.concatenate(split2(matrix), axis=1)
        projected = dot(matrix2, jnp.concatenate([lat] * 2, axis=0)) * rstd + shift
        ones = (iota((8, TOK), 0) == 0).astype(F32)
        for h in range(2):
            at = h * 3 * HD
            query = head_norm(projected[at : at + HD], gains[:, 0:1]) * SCORE
            keys = head_norm(projected[at + HD : at + 2 * HD], gains[:, 1:2])
            values = projected[at + 2 * HD : at + 3 * HD]
            qb[h] = query.astype(BF)
            kb[h] = keys.T.astype(BF)
            vb[h] = jnp.concatenate([values, ones], axis=0).astype(BF)

    def attend_frame(j):
        chunk = 256

        @pl.loop(0, 2 * TOK // chunk)
        def _(i):
            h = i // (TOK // chunk)
            columns = pl.ds(pl.multiple_of(i % (TOK // chunk) * chunk, chunk), chunk)
            scores = dot(kb[h], qb[h, :, columns])
            weighted = dot(vb[h], jnp.exp2(scores).astype(BF))
            att_f[pl.ds(pl.multiple_of(h * HD, 8), HD), columns] = weighted[:HD] / weighted[HD : HD + 1]

        att[j] = att_f[...].astype(BF)

    def share_rows(share):
        return pl.ds(pl.multiple_of(share * 144, 16), 144)

    def share_columns(share):
        return pl.ds(pl.multiple_of(share * OWN, OWN), OWN)

    def att_copy(j, k):
        peer = space_peer(k)
        return push(
            att.at[j, :, share_columns(peer)], att_in.at[j, share_rows(s), :],
            att_ssem.at[j, k], att_rsem.at[j, s], (f, peer),
        )

    def att_wait(j, k):
        origin = space_peer(k)
        push(
            att.at[j, :, share_columns(origin)], att_in.at[j, share_rows(origin), :],
            att_ssem.at[j, k], att_rsem.at[j, origin], (f, origin),
        ).wait_recv()

    def att_own(j):
        return pltpu.make_async_copy(
            att.at[j, :, share_columns(s)], att_in.at[j, share_rows(s), :], own_sem.at[1 + j]
        )

    for j in range(2):
        project_frame(j)
        attend_frame(j)

        @pl.loop(1, NS)
        def _(k):
            att_copy(j, k).start()

        att_own(j).start()
        if j == 0:
            take(0, 4, 7)
        else:
            take(6, 10)
            take(1)
            take_core(1, 8)

    for j in range(2):
        att_own(j).wait()

        @pl.loop(1, NS)
        def _(k):
            att_wait(j, k)

    row, column = iota((16 * NF, 2 * OWN), 0), iota((16 * NF, 2 * OWN), 1)
    matching = column == row % 8 // SUB * OWN + row // 16 * SUB + row % SUB
    upper = row // 8 % 2 == 0
    own_lats = jnp.concatenate([lat_send[0], lat_send[1]], axis=1)
    tail = jnp.concatenate([own_lats, jnp.zeros((WIDE - D // 2 - PATCH, 2 * OWN), BF)], axis=0)
    both = jnp.concatenate([att_in[0], att_in[1]], axis=1)
    gathered = jnp.zeros((16 * NF, WIDE), F32)
    for h in range(2):
        piece = jnp.concatenate([both[h * (D // 2) : (h + 1) * (D // 2)], tail], axis=0)
        gathered += dot((matching & (upper == (h == 0))).astype(BF), piece, NT)
    send[...] = gathered.astype(BF)

    def row_copy(k):
        peer = frame_peer(k)
        return push(
            send.at[pl.ds(pl.multiple_of(peer * 16, 16), 16), :],
            recv.at[pl.ds(pl.multiple_of(f * 16, 16), 16), :],
            row_ssem.at[k], row_rsem.at[f], (peer, s),
        )

    def row_wait(k):
        origin = frame_peer(k)
        rows = pl.ds(pl.multiple_of(origin * 16, 16), 16)
        push(send.at[rows, :], recv.at[rows, :], row_ssem.at[k], row_rsem.at[origin], (origin, s)).wait_recv()

    @pl.loop(1, NF)
    def _(k):
        row_copy(k).start()

    own_rows = pl.ds(pl.multiple_of(f * 16, 16), 16)
    own_copy = pltpu.make_async_copy(send.at[own_rows, :], recv.at[own_rows, :], own_sem.at[3])
    own_copy.start()

    @pl.loop(1, NF)
    def _(k):
        step_copy(k, frame_peer(k)).wait_recv()

    wanted = jnp.concatenate([step_rows[0:ROWS, :]] * 8, axis=1) * 8.0
    slots = iota((ROWS, 8 * STEPS), 1).astype(F32)
    for kind in range(6):
        mods[kind] = dot((wanted + (kind + 2.0) == slots).astype(BF), table[...])

    take(2, 5)
    take(3)
    take(4, 9)
    take(7, 11)
    take(5)
    take(10)
    take(8, 12)
    take(11)
    take(9, 13)

    own_copy.wait()

    @pl.loop(1, NF)
    def _(k):
        row_wait(k)

    take(12)
    take(13)

    for i in (0, 2, 3, 4, 5, 6, 7, 8, 9, 10, 11, 12, 13):
        take_core(i)

    row, column = iota((ROWS, 16 * NF), 0), iota((ROWS, 16 * NF), 1)
    halves = [
        dot((column == row // 8 * 16 + h * 8 + row % 8).astype(BF), recv[...]) for h in range(2)
    ]
    hidden = dot(halves[0][:, D // 2 : D // 2 + PATCH].astype(BF), embed[...])
    output = jnp.zeros((ROWS, D), F32)
    for i in range(NS):
        at = i % 4 * 144
        output += dot(halves[i // 4][:, at : at + 144].astype(BF), weights[i, OUT_S:QKV_T, :])
    hidden += mods[0] * output

    ready = (layer_norm(hidden) * (1.0 + mods[2]) + mods[1]).astype(BF)
    for i in range(NS):
        proj[i] = dot(weights[i, QKV_T:OUT_T, :], ready, NT)
    same = iota((ROWS, ROWS), 0) % SUB == iota((ROWS, ROWS), 1) % SUB
    ones = (iota((8, ROWS), 0) == 0).astype(F32)

    @pl.loop(0, 2 * NS)
    def _(i):
        share, at = i // 2, pl.multiple_of(i % 2 * 3 * HD, 8)
        query = head_norm(proj[share, pl.ds(at, HD), :], gains[:, 2:3]) * SCORE
        keys = head_norm(proj[share, pl.ds(at + HD, HD), :], gains[:, 3:4])
        values = jnp.concatenate([proj[share, pl.ds(at + 2 * HD, HD), :], ones], axis=0).astype(BF)
        scores = dot(keys.T.astype(BF), query.astype(BF))
        weighted = dot(values, jnp.where(same, jnp.exp2(scores), 0.0).astype(BF))
        att_t[pl.ds(pl.multiple_of(i * HD, 8), HD), :] = weighted[:HD] / weighted[HD : HD + 1]

    output = jnp.zeros((ROWS, D), F32)
    for i in range(NS):
        output += dot(att_t[144 * i : 144 * i + 144, :].T.astype(BF), weights[i, OUT_T : OUT_T + 144, :])
    hidden += mods[3] * output
    ready = (layer_norm(hidden) * (1.0 + mods[5]) + mods[4]).astype(BF)
    vel_send[0:ROWS, 0:PATCH] = dot(ready, final[...])

    def vel_copy(k):
        peer = frame_peer(k)
        return push(
            vel_send.at[pl.ds(pl.multiple_of(peer * 8, 8), 16), :], vel_recv.at[f],
            vel_ssem.at[k], vel_rsem.at[f], (peer, s),
        )

    def vel_wait(k):
        origin = frame_peer(k)
        push(
            vel_send.at[pl.ds(pl.multiple_of(origin * 8, 8), 16), :], vel_recv.at[origin],
            vel_ssem.at[k], vel_rsem.at[origin], (origin, s),
        ).wait_recv()

    @pl.loop(1, NF)
    def _(k):
        vel_copy(k).start()

    own_vel = pltpu.make_async_copy(
        vel_send.at[pl.ds(pl.multiple_of(f * 8, 8), 16), :], vel_recv.at[f], own_sem.at[4]
    )
    own_vel.start()
    next_copy().wait_recv()
    own_vel.wait()

    @pl.loop(1, NF)
    def _(k):
        vel_wait(k)

    turned = vel_recv[...].reshape(16 * NF, 128).T[0:PATCH, :]
    turned3 = jnp.concatenate(split3(turned), axis=0)
    row, column = iota((16 * NF, OWN), 0), iota((16 * NF, OWN), 1)
    updated = []
    for j in range(3):
        spread = dot(turned3, (row == column // SUB * 16 + j * SUB + column % SUB).astype(BF))
        found = spread[0:16] + spread[16:32] + spread[32:48]
        index = step_rows[pl.ds(f * 8 + j * SUB, 1), :]
        size = level(index + 1.0) - level(index)
        if j < 2:
            velocity[j] = found
        updated.append((latents[j] if j < 2 else lat_next[...]) - size * found)
    queue[0] = updated[1]
    queue[1] = jnp.where(f == NF - 1, noise[...], updated[2])

    for j in range(2):

        @pl.loop(1, NS)
        def _(k):
            att_copy(j, k).wait_send()

    @pl.loop(1, NS)
    def _(k):
        lat_copy(k).wait_send()

    @pl.loop(1, NF)
    def _(k):
        step_copy(k, f).wait_send()
        row_copy(k).wait_send()
        vel_copy(k).wait_send()

    next_copy().wait_send()
    for i in range(14):
        hop(i, *hop_source(i)).wait_send()
        core_copy(i, c).wait_send()


def local(
    latents, time_index, fresh_noise, modulation_table, embed_weight, spatial_qkv, spatial_out,
    temporal_qkv, temporal_out, final_weight, spatial_gain, temporal_gain,
):
    gains = jnp.concatenate([spatial_gain, temporal_gain], axis=0).T
    dma = pltpu.SemaphoreType.DMA
    vmem = pl.BlockSpec(memory_space=pltpu.VMEM)
    smem = pl.BlockSpec(memory_space=pltpu.SMEM)
    return pl.pallas_call(
        kernel,
        out_shape=(
            jax.ShapeDtypeStruct(latents.shape, F32),
            jax.ShapeDtypeStruct(latents.shape, F32),
        ),
        in_specs=[vmem, smem] + [vmem] * 9,
        out_specs=(vmem, vmem),
        scratch_shapes=[
            pltpu.VMEM((NS, SHARD, D), BF),
            pltpu.VMEM((2, PATCH, OWN), BF),
            pltpu.VMEM((NS, 2, PATCH, OWN), BF),
            pltpu.VMEM((PATCH, OWN), F32),
            pltpu.VMEM((ROWS + 8, 128), F32),
            pltpu.VMEM((2, HD, TOK), BF),
            pltpu.VMEM((2, TOK, HD), BF),
            pltpu.VMEM((2, HD + 8, TOK), BF),
            pltpu.VMEM((144, TOK), F32),
            pltpu.VMEM((2, 144, TOK), BF),
            pltpu.VMEM((2, D, OWN), BF),
            pltpu.VMEM((16 * NF, WIDE), BF),
            pltpu.VMEM((16 * NF, WIDE), BF),
            pltpu.VMEM((6, ROWS, D), F32),
            pltpu.VMEM((NS, 432, ROWS), F32),
            pltpu.VMEM((D, ROWS), F32),
            pltpu.VMEM((ROWS + 8, 128), F32),
            pltpu.VMEM((NF, 16, 128), F32),
            dma((NS,)),
            dma((NS,)),
            dma((2,)),
            dma((NF,)),
            dma((NF,)),
            dma((14,)),
            dma((14,)),
            dma((14,)),
            dma((14,)),
            dma((2, NS)),
            dma((2, NS)),
            dma((NF,)),
            dma((NF,)),
            dma((NF,)),
            dma((NF,)),
            dma((5,)),
        ],
        compiler_params=pltpu.CompilerParams(
            collective_id=0, has_side_effects=True, vmem_limit_bytes=60 * 1024 * 1024
        ),
    )(
        latents, time_index, fresh_noise, modulation_table.reshape(STEPS * 8, D), embed_weight,
        spatial_qkv, spatial_out, temporal_qkv, temporal_out, final_weight, gains,
    )


def solution(mesh):
    return jax.shard_map(
        local,
        mesh=mesh,
        in_specs=(
            P("frame", None, "space"),
            P("frame"),
            P(None, "space"),
            P(),
            P(),
            P(None, "space"),
            P("space", None),
            P(None, "space"),
            P("space", None),
            P(),
            P(),
            P(),
        ),
        out_specs=(P("frame", None, "space"), P("frame", None, "space")),
        check_vma=False,
    )
```

```python
import jax
import jax.numpy as jnp
from jax import lax
from jax.experimental import pallas as pl
from jax.experimental.pallas import tpu as pltpu
from jax.sharding import PartitionSpec as P

HD = 72
D = 1152
NF = 32
NS = 8
STEPS = 128
PATCH = 16
TOK = 1024
OWN = 128
SUB = 4
SHARD = 768
PART = SHARD // 8
HOPS = 24
OUT_S, QKV_T, OUT_T = 0, 144, 576
ROWS = 2 * SUB * NF
WIDE = 640
EPS = 1e-6
LOG2E = 1.4426950408889634
SCORE = HD ** -0.5 * LOG2E
BF = jnp.bfloat16
F32 = jnp.float32

NN = (((1,), (0,)), ((), ()))
NT = (((1,), (1,)), ((), ()))


def dot(a, b, dims=NN, precision=None):
    return lax.dot_general(a, b, dims, preferred_element_type=F32, precision=precision)


def iota(shape, axis):
    return lax.broadcasted_iota(jnp.int32, shape, axis)


def split2(a):
    high = a.astype(BF)
    return high, (a - high.astype(F32)).astype(BF)


def split3(a):
    high = a.astype(BF)
    rest = a - high.astype(F32)
    mid = rest.astype(BF)
    return high, mid, (rest - mid.astype(F32)).astype(BF)


def layer_norm(a):
    center = a - jnp.mean(a, axis=-1, keepdims=True)
    spread = jnp.mean(center * center, axis=-1, keepdims=True)
    return center * lax.rsqrt(spread + EPS)


def head_norm(a, gain):
    return a * lax.rsqrt(jnp.mean(a * a, axis=0, keepdims=True) + EPS) * gain


def level(index):
    fraction = index * (1.0 / STEPS)
    return 3.0 * fraction / (1.0 + 2.0 * fraction)


def kernel(
    latents, steps, noise, table_in, embed, qkv_s_in, out_s, qkv_t, out_t, final, gain_s, gain_t,
    velocity, queue,
    table, qkv_s, weights, lat_send, lat_all, lat_next, step_rows, qb, kb, vb, att_f, att, att_in, send, recv,
    mods, proj, att_t, vel_send, vel_recv,
    lat_ssem, lat_rsem, next_sem, step_ssem, step_rsem, dir_ssem, dir_rsem, core_ssem, core_rsem,
    att_ssem, att_rsem, row_ssem, row_rsem, vel_ssem, vel_rsem, own_sem, load_sem,
):
    f = lax.axis_index("frame")
    s = lax.axis_index("space")
    c = f % 2
    z = f // 2 % 8
    yl = f // 16
    x = s // 2
    yh = s % 2

    def frame_peer(k):
        return lax.rem(f + k, NF)

    def space_peer(k):
        return lax.rem(s + k, NS)

    step = 1 - 2 * c
    to_x = (f, lax.rem(x + step + 4, 4) * 2 + yh)
    to_core = (f + step, s)
    to_cross = (lax.rem(f + 16, NF), 2 * x + 1 - yh)
    to_side = (lax.rem(f + 16, NF), s)
    to_z = (yl * 16 + lax.rem(z + step + 8, 8) * 2 + c, s)

    barrier = pltpu.get_barrier_semaphore()

    def greet(target):
        pl.semaphore_signal(barrier, inc=1, device_id=target, device_id_type=pl.DeviceIdType.MESH)

    @pl.loop(1, NF)
    def _(k):
        greet((frame_peer(k), s))

    @pl.loop(1, NS)
    def _(k):
        greet((f, space_peer(k)))

    greet(to_cross)

    def push(src, dst, ssem, rsem, target):
        return pltpu.make_async_remote_copy(
            src_ref=src, dst_ref=dst, send_sem=ssem, recv_sem=rsem,
            device_id=target, device_id_type=pl.DeviceIdType.MESH,
        )

    loads = [
        pltpu.make_async_copy(out_s, weights.at[s, OUT_S:QKV_T, :], load_sem.at[0]),
        pltpu.make_async_copy(qkv_t, weights.at[s, QKV_T:OUT_T, :], load_sem.at[1]),
        pltpu.make_async_copy(out_t, weights.at[s, OUT_T : OUT_T + 144, :], load_sem.at[2]),
        pltpu.make_async_copy(qkv_s_in, qkv_s, load_sem.at[3]),
        pltpu.make_async_copy(table_in, table, load_sem.at[4]),
    ]
    for load in loads:
        load.start()
    for j in range(2):
        lat_send[j] = latents[j].astype(BF)
    weights[s, OUT_T + 144 :, :] = jnp.zeros((SHARD - OUT_T - 144, D), BF)
    half = iota((8, 128), 0) < SUB
    own_steps = jnp.where(half, steps[0], steps[1]).astype(F32)
    step_rows[pl.ds(pl.multiple_of(f * 8, 8), 8), :] = own_steps
    step_rows[ROWS:, :] = jnp.zeros((8, 128), F32)
    vel_send[NF:] = jnp.zeros((1, 1, 128), F32)

    pl.semaphore_wait(barrier, NF + NS - 1)

    def lat_copy(k):
        return push(lat_send, lat_all.at[s], lat_ssem.at[k], lat_rsem.at[s], (f, space_peer(k)))

    def lat_wait(k):
        origin = space_peer(k)
        push(lat_send, lat_all.at[origin], lat_ssem.at[k], lat_rsem.at[origin], (f, origin)).wait_recv()

    def next_copy():
        return push(latents.at[0], lat_next, next_sem.at[0], next_sem.at[1], (frame_peer(NF - 1), s))

    def step_copy(k, row):
        rows = pl.ds(pl.multiple_of(row * 8, 8), 8)
        return push(
            step_rows.at[rows], step_rows.at[rows], step_ssem.at[k], step_rsem.at[row], (frame_peer(k), s)
        )

    @pl.loop(1, NS)
    def _(k):
        lat_copy(k).start()

    own_lat = pltpu.make_async_copy(lat_send, lat_all.at[s], own_sem.at[0])
    own_lat.start()

    def quarter(m):
        return lax.rem(yl + m // 2, 2) * 2 + lax.rem(z + m % 2, 2)

    def near(j, who):
        turn = 1 - 2 * who
        return (x, lax.rem(x - turn + 4, 4), lax.rem(x + turn + 4, 4), lax.rem(x + 2, 4))[j]

    def block(i, who):
        j = i % 4
        if i < 4:
            return near(1, who) * 2 + yh, quarter(j) * 2, 2
        if i < 8:
            return near(3, who) * 2 + yh, quarter(j) * 2 + who, 1
        return near(j, who) * 2 + 1 - yh, quarter((2, 0, 3, 1)[i // 4 - 2]) * 2 + who, 1

    def hop_source(i):
        if i < 4:
            return s, quarter(i) * 2, 2
        if i < 8:
            share, part, _ = block(i - 4, c)
            return share, part + c, 1
        if i < 12:
            return near(i - 8, c) * 2 + yh, quarter(0) * 2 + c, 1
        return block(i - 4 if i < 16 else i - 8, c)

    def place(share, part, count):
        return weights.at[share, pl.ds(pl.multiple_of(part * PART, PART), PART * count), :]

    def hop(i, spot):
        target = to_x if i < 8 else to_cross if i < 12 else to_side if i < 16 else to_z
        return push(spot, spot, dir_ssem.at[i], dir_rsem.at[i], target)

    def hop_start(i):
        hop(i, place(*hop_source(i))).start()

    def core_copy(i, who):
        spot = place(*block(i, who))
        return push(spot, spot, core_ssem.at[i], core_rsem.at[i], to_core)

    then = {0: (9, 4, 2), 1: (5, 3), 2: (6,), 3: (7,), 4: (11,)}
    for j in range(4):
        then[8 + j] = (16 + j, 12 + j)
        then[12 + j] = (20 + j,)

    def take(*hops):
        for i in hops:
            hop(i, place(*block(i, c))).wait_recv()
            core_copy(i, c).start()
            for k in then.get(i, ()):
                hop_start(k)

    for load in loads[:3]:
        load.wait()
    hop_start(0)
    hop_start(8)
    hop_start(1)

    @pl.loop(1, NF)
    def _(k):
        step_copy(k, f).start()

    next_copy().start()

    base = embed[...].astype(F32)
    center = base - jnp.mean(base, axis=1, keepdims=True)
    gram = dot(center, center, NT, lax.Precision.HIGHEST) * (1.0 / D)
    gram3 = jnp.concatenate(split3(gram), axis=1)
    eye = (iota((HD, HD), 0) == iota((HD, HD), 1)).astype(F32)
    gains_s = dot(eye, gain_s[...], NT, lax.Precision.HIGHEST)
    gains_t = dot(eye, gain_t[...], NT, lax.Precision.HIGHEST)
    loads[4].wait()
    slot = iota((16, 8 * STEPS), 1) - iota((16, 8 * STEPS), 0) % 8
    wanted = jnp.where(iota((16, 8 * STEPS), 0) < 8, steps[0], steps[1]) * 8
    both_mods = dot((slot == wanted).astype(BF), table[...])
    own_mods = [both_mods[:8], both_mods[8:]]
    parts = []
    for j in range(2):
        parts.extend(split2(center * (1.0 + own_mods[j][1:2, :])))
    parts.append(jnp.concatenate(own_mods, axis=0).astype(BF))
    stack = jnp.concatenate(parts, axis=0)
    loads[3].wait()
    mixed = dot(qkv_s[...], stack, NT)

    own_lat.wait()

    @pl.loop(1, NS)
    def _(k):
        lat_wait(k)

    def project_frame(j):
        lat = jnp.concatenate([lat_all[i, j] for i in range(NS)], axis=1)
        lat32 = lat.astype(F32)
        spread = jnp.sum(lat32 * dot(gram3, jnp.concatenate([lat] * 3, axis=0)), axis=0, keepdims=True)
        rstd = lax.rsqrt(jnp.maximum(spread, 0.0) + EPS)
        matrix = mixed[:, 32 * j : 32 * j + 16] + mixed[:, 32 * j + 16 : 32 * j + 32]
        shift = mixed[:, 64 + 8 * j : 65 + 8 * j]
        matrix2 = jnp.concatenate(split2(matrix), axis=1)
        projected = dot(matrix2, jnp.concatenate([lat] * 2, axis=0)) * rstd + shift
        ones = (iota((8, TOK), 0) == 0).astype(F32)
        for h in range(2):
            at = h * 3 * HD
            query = head_norm(projected[at : at + HD], gains_s[:, 0:1]) * SCORE
            keys = head_norm(projected[at + HD : at + 2 * HD], gains_s[:, 1:2])
            values = projected[at + 2 * HD : at + 3 * HD]
            qb[h] = query.astype(BF)
            kb[h] = keys.T.astype(BF)
            vb[h] = jnp.concatenate([values, ones], axis=0).astype(BF)

    def attend_head(h):
        chunk = 256

        @pl.loop(0, TOK // chunk)
        def _(i):
            columns = pl.ds(pl.multiple_of(i * chunk, chunk), chunk)
            scores = dot(kb[h], qb[h, :, columns])
            weighted = dot(vb[h], jnp.exp2(scores).astype(BF))
            att_f[h * HD : (h + 1) * HD, columns] = weighted[:HD] / weighted[HD : HD + 1]

    def share_rows(share):
        return pl.ds(pl.multiple_of(share * 144, 16), 144)

    def share_columns(share):
        return pl.ds(pl.multiple_of(share * OWN, OWN), OWN)

    def att_copy(j, k):
        peer = space_peer(k)
        return push(
            att.at[j, :, share_columns(peer)], att_in.at[j, share_rows(s), :],
            att_ssem.at[j, k], att_rsem.at[j, s], (f, peer),
        )

    def att_wait(j, k):
        origin = space_peer(k)
        push(
            att.at[j, :, share_columns(origin)], att_in.at[j, share_rows(origin), :],
            att_ssem.at[j, k], att_rsem.at[j, origin], (f, origin),
        ).wait_recv()

    def att_own(j):
        return pltpu.make_async_copy(
            att.at[j, :, share_columns(s)], att_in.at[j, share_rows(s), :], own_sem.at[1 + j]
        )

    for j in range(2):
        project_frame(j)
        if j == 0:
            take(0, 8)
            core_copy(0, 1 - c).wait_recv()
            hop_start(10)
        attend_head(0)
        take(*((1, 16) if j == 0 else (17, 20, 10, 2)))
        attend_head(1)
        att[j] = att_f[...].astype(BF)

        @pl.loop(1, NS)
        def _(k):
            att_copy(j, k).start()

        att_own(j).start()
        take(*((12, 9, 4) if j == 0 else (13, 5, 11)))

    for j in range(2):
        att_own(j).wait()

        @pl.loop(1, NS)
        def _(k):
            att_wait(j, k)

    take(18, 14, 3)

    row, column = iota((16 * NF, 2 * OWN), 0), iota((16 * NF, 2 * OWN), 1)
    matching = column == row % 8 // SUB * OWN + row // 16 * SUB + row % SUB
    upper = row // 8 % 2 == 0
    own_lats = jnp.concatenate([lat_send[0], lat_send[1]], axis=1)
    tail = jnp.concatenate([own_lats, jnp.zeros((WIDE - D // 2 - PATCH, 2 * OWN), BF)], axis=0)
    both = jnp.concatenate([att_in[0], att_in[1]], axis=1)
    gathered = jnp.zeros((16 * NF, WIDE), F32)
    for h in range(2):
        piece = jnp.concatenate([both[h * (D // 2) : (h + 1) * (D // 2)], tail], axis=0)
        gathered += dot((matching & (upper == (h == 0))).astype(BF), piece, NT)
    send[...] = gathered.astype(BF)

    def row_copy(k):
        peer = frame_peer(k)
        return push(
            send.at[pl.ds(pl.multiple_of(peer * 16, 16), 16), :],
            recv.at[pl.ds(pl.multiple_of(f * 16, 16), 16), :],
            row_ssem.at[k], row_rsem.at[f], (peer, s),
        )

    def row_wait(k):
        origin = frame_peer(k)
        rows = pl.ds(pl.multiple_of(origin * 16, 16), 16)
        push(send.at[rows, :], recv.at[rows, :], row_ssem.at[k], row_rsem.at[origin], (origin, s)).wait_recv()

    @pl.loop(1, NF)
    def _(k):
        row_copy(k).start()

    own_rows = pl.ds(pl.multiple_of(f * 16, 16), 16)
    own_copy = pltpu.make_async_copy(send.at[own_rows, :], recv.at[own_rows, :], own_sem.at[3])
    own_copy.start()

    take(21, 19, 6)

    @pl.loop(1, NF)
    def _(k):
        step_copy(k, frame_peer(k)).wait_recv()

    wanted = jnp.concatenate([step_rows[0:ROWS, :]] * 8, axis=1) * 8.0
    slots = iota((ROWS, 8 * STEPS), 1).astype(F32)
    for kind in range(6):
        mods[kind] = dot((wanted + (kind + 2.0) == slots).astype(BF), table[...])

    take(15, 22, 7, 23)
    own_copy.wait()

    @pl.loop(1, NF)
    def _(k):
        row_wait(k)

    for i in range(1, HOPS):
        core_copy(i, 1 - c).wait_recv()

    row, column = iota((ROWS, 16 * NF), 0), iota((ROWS, 16 * NF), 1)
    halves = [
        dot((column == row // 8 * 16 + h * 8 + row % 8).astype(BF), recv[...]) for h in range(2)
    ]
    hidden = dot(halves[0][:, D // 2 : D // 2 + PATCH].astype(BF), embed[...])
    output = jnp.zeros((ROWS, D), F32)
    for i in range(NS):
        at = i % 4 * 144
        output += dot(halves[i // 4][:, at : at + 144].astype(BF), weights[i, OUT_S:QKV_T, :])
    hidden += mods[0] * output

    ready = (layer_norm(hidden) * (1.0 + mods[2]) + mods[1]).astype(BF)
    for i in range(NS):
        proj[i] = dot(weights[i, QKV_T:OUT_T, :], ready, NT)
    same = iota((ROWS, ROWS), 0) % SUB == iota((ROWS, ROWS), 1) % SUB
    ones = (iota((8, ROWS), 0) == 0).astype(F32)

    @pl.loop(0, NS // 2)
    def _(i):
        for n in range(4):
            share, at = 2 * i + n // 2, n % 2 * 3 * HD
            query = head_norm(proj[share, at : at + HD, :], gains_t[:, 0:1]) * SCORE
            keys = head_norm(proj[share, at + HD : at + 2 * HD, :], gains_t[:, 1:2])
            values = jnp.concatenate([proj[share, at + 2 * HD : at + 3 * HD, :], ones], axis=0).astype(BF)
            scores = dot(keys.T.astype(BF), query.astype(BF))
            weighted = dot(values, jnp.where(same, jnp.exp2(scores), 0.0).astype(BF))
            rows = pl.ds(pl.multiple_of((4 * i + n) * HD, 8), HD)
            att_t[rows, :] = weighted[:HD] / weighted[HD : HD + 1]

    output = jnp.zeros((ROWS, D), F32)
    for i in range(NS):
        output += dot(att_t[144 * i : 144 * i + 144, :].T.astype(BF), weights[i, OUT_T : OUT_T + 144, :])
    hidden += mods[3] * output
    ready = (layer_norm(hidden) * (1.0 + mods[5]) + mods[4]).astype(BF)
    wide = dot(ready, jnp.concatenate([final[...]] * 8, axis=0), NT)
    wide = jnp.where(iota((ROWS, 128), 0) % 8 == iota((ROWS, 128), 1) // PATCH, wide, 0.0)
    vel_send[0:NF] = jnp.sum(wide.reshape(NF, 8, 128), axis=1, keepdims=True)

    def vel_copy(k):
        peer = frame_peer(k)
        return push(
            vel_send.at[pl.ds(peer, 2)], vel_recv.at[f],
            vel_ssem.at[k], vel_rsem.at[f], (peer, s),
        )

    def vel_wait(k):
        origin = frame_peer(k)
        push(
            vel_send.at[pl.ds(origin, 2)], vel_recv.at[origin],
            vel_ssem.at[k], vel_rsem.at[origin], (origin, s),
        ).wait_recv()

    @pl.loop(1, NF)
    def _(k):
        vel_copy(k).start()

    own_vel = pltpu.make_async_copy(
        vel_send.at[pl.ds(f, 2)], vel_recv.at[f], own_sem.at[4]
    )
    own_vel.start()
    next_copy().wait_recv()
    own_vel.wait()

    @pl.loop(1, NF)
    def _(k):
        vel_wait(k)

    turned = [vel_recv[:, i, 0, :].T for i in range(2)]
    row, column = iota((NF, OWN), 0), iota((NF, OWN), 1)
    updated = []
    for j in range(3):
        found = jnp.zeros((PATCH, OWN), F32)
        for t in range(SUB):
            at = (j % 2 * SUB + t) * PATCH
            mine = jnp.concatenate(split3(turned[j // 2][at : at + PATCH]), axis=0)
            spread = dot(mine, (column == SUB * row + t).astype(BF))
            found += spread[0:16] + spread[16:32] + spread[32:48]
        index = step_rows[pl.ds(f * 8 + j * SUB, 1), :]
        size = level(index + 1.0) - level(index)
        if j < 2:
            velocity[j] = found
        updated.append((latents[j] if j < 2 else lat_next[...]) - size * found)
    queue[0] = updated[1]
    queue[1] = jnp.where(f == NF - 1, noise[...], updated[2])

    for j in range(2):

        @pl.loop(1, NS)
        def _(k):
            att_copy(j, k).wait_send()

    @pl.loop(1, NS)
    def _(k):
        lat_copy(k).wait_send()

    @pl.loop(1, NF)
    def _(k):
        step_copy(k, f).wait_send()
        row_copy(k).wait_send()
        vel_copy(k).wait_send()

    next_copy().wait_send()
    for i in range(HOPS):
        hop(i, place(*hop_source(i))).wait_send()
        core_copy(i, c).wait_send()


def local(
    latents, time_index, fresh_noise, modulation_table, embed_weight, spatial_qkv, spatial_out,
    temporal_qkv, temporal_out, final_weight, spatial_gain, temporal_gain,
):
    dma = pltpu.SemaphoreType.DMA
    vmem = pl.BlockSpec(memory_space=pltpu.VMEM)
    hbm = pl.BlockSpec(memory_space=pl.ANY)
    smem = pl.BlockSpec(memory_space=pltpu.SMEM)
    return pl.pallas_call(
        kernel,
        out_shape=(
            jax.ShapeDtypeStruct(latents.shape, F32),
            jax.ShapeDtypeStruct(latents.shape, F32),
        ),
        in_specs=[vmem, smem, vmem, hbm, vmem, hbm, hbm, hbm, hbm, vmem, vmem, vmem],
        out_specs=(vmem, vmem),
        scratch_shapes=[
            pltpu.VMEM((8 * STEPS, D), BF),
            pltpu.VMEM((432, D), BF),
            pltpu.VMEM((NS, SHARD, D), BF),
            pltpu.VMEM((2, PATCH, OWN), BF),
            pltpu.VMEM((NS, 2, PATCH, OWN), BF),
            pltpu.VMEM((PATCH, OWN), F32),
            pltpu.VMEM((ROWS + 8, 128), F32),
            pltpu.VMEM((2, HD, TOK), BF),
            pltpu.VMEM((2, TOK, HD), BF),
            pltpu.VMEM((2, HD + 8, TOK), BF),
            pltpu.VMEM((144, TOK), F32),
            pltpu.VMEM((2, 144, TOK), BF),
            pltpu.VMEM((2, D, OWN), BF),
            pltpu.VMEM((16 * NF, WIDE), BF),
            pltpu.VMEM((16 * NF, WIDE), BF),
            pltpu.VMEM((6, ROWS, D), F32),
            pltpu.VMEM((NS, 432, ROWS), F32),
            pltpu.VMEM((D, ROWS), F32),
            pltpu.VMEM((NF + 1, 1, 128), F32),
            pltpu.VMEM((NF, 2, 1, 128), F32),
            dma((NS,)),
            dma((NS,)),
            dma((2,)),
            dma((NF,)),
            dma((NF,)),
            dma((HOPS,)),
            dma((HOPS,)),
            dma((HOPS,)),
            dma((HOPS,)),
            dma((2, NS)),
            dma((2, NS)),
            dma((NF,)),
            dma((NF,)),
            dma((NF,)),
            dma((NF,)),
            dma((5,)),
            dma((5,)),
        ],
        compiler_params=pltpu.CompilerParams(
            collective_id=0, has_side_effects=True, vmem_limit_bytes=60 * 1024 * 1024
        ),
    )(
        latents, time_index, fresh_noise, modulation_table.reshape(STEPS * 8, D), embed_weight,
        spatial_qkv.T, spatial_out, temporal_qkv.T, temporal_out, final_weight.T, spatial_gain, temporal_gain,
    )


def solution(mesh):
    return jax.shard_map(
        local,
        mesh=mesh,
        in_specs=(
            P("frame", None, "space"),
            P("frame"),
            P(None, "space"),
            P(),
            P(),
            P(None, "space"),
            P("space", None),
            P(None, "space"),
            P("space", None),
            P(),
            P(),
            P(),
        ),
        out_specs=(P("frame", None, "space"), P("frame", None, "space")),
        check_vma=False,
    )
```

```python
import jax
import jax.numpy as jnp
from jax import lax
from jax.experimental import pallas as pl
from jax.experimental.pallas import tpu as pltpu
from jax.sharding import PartitionSpec as P

HD = 72
D = 1152
NF = 32
NS = 8
STEPS = 128
PATCH = 16
TOK = 1024
OWN = 128
SUB = 4
SHARD = 768
PART = SHARD // 8
HOPS = 24
OUT_S, QKV_T, OUT_T = 0, 144, 576
ROWS = 2 * SUB * NF
WIDE = 640
EPS = 1e-6
LOG2E = 1.4426950408889634
SCORE = HD ** -0.5 * LOG2E
BF = jnp.bfloat16
F32 = jnp.float32

NN = (((1,), (0,)), ((), ()))
NT = (((1,), (1,)), ((), ()))


def dot(a, b, dims=NN, precision=None):
    return lax.dot_general(a, b, dims, preferred_element_type=F32, precision=precision)


def iota(shape, axis):
    return lax.broadcasted_iota(jnp.int32, shape, axis)


def split2(a):
    high = a.astype(BF)
    return high, (a - high.astype(F32)).astype(BF)


def split3(a):
    high = a.astype(BF)
    rest = a - high.astype(F32)
    mid = rest.astype(BF)
    return high, mid, (rest - mid.astype(F32)).astype(BF)


def layer_norm(a):
    center = a - jnp.mean(a, axis=-1, keepdims=True)
    spread = jnp.mean(center * center, axis=-1, keepdims=True)
    return center * lax.rsqrt(spread + EPS)


def head_norm(a, gain):
    return a * lax.rsqrt(jnp.mean(a * a, axis=0, keepdims=True) + EPS) * gain


def level(index):
    fraction = index * (1.0 / STEPS)
    return 3.0 * fraction / (1.0 + 2.0 * fraction)


def kernel(
    latents, steps, noise, table_in, embed, qkv_s_in, out_s, qkv_t, out_t, final, gain_s, gain_t,
    result,
    table, qkv_s, weights, lat_send, lat_all, lat_next, step_rows, qb, kb, vb, att_f, att, att_in, send, recv,
    mods, proj, att_t, vel_send, vel_recv,
    lat_ssem, lat_rsem, next_sem, step_ssem, step_rsem, dir_ssem, dir_rsem, core_ssem, core_rsem,
    att_ssem, att_rsem, row_ssem, row_rsem, vel_ssem, vel_rsem, own_sem, load_sem,
):
    f = lax.axis_index("frame")
    s = lax.axis_index("space")
    c = f % 2
    z = f // 2 % 8
    yl = f // 16
    x = s // 2
    yh = s % 2

    def frame_peer(k):
        return lax.rem(f + k, NF)

    def space_peer(k):
        return lax.rem(s + k, NS)

    step = 1 - 2 * c
    to_x = (f, lax.rem(x + step + 4, 4) * 2 + yh)
    to_core = (f + step, s)
    to_cross = (lax.rem(f + 16, NF), 2 * x + 1 - yh)
    to_side = (lax.rem(f + 16, NF), s)
    to_z = (yl * 16 + lax.rem(z + step + 8, 8) * 2 + c, s)

    barrier = pltpu.get_barrier_semaphore()

    def greet(target):
        pl.semaphore_signal(barrier, inc=1, device_id=target, device_id_type=pl.DeviceIdType.MESH)

    @pl.loop(1, NF)
    def _(k):
        greet((frame_peer(k), s))

    @pl.loop(1, NS)
    def _(k):
        greet((f, space_peer(k)))

    greet(to_cross)

    def push(src, dst, ssem, rsem, target):
        return pltpu.make_async_remote_copy(
            src_ref=src, dst_ref=dst, send_sem=ssem, recv_sem=rsem,
            device_id=target, device_id_type=pl.DeviceIdType.MESH,
        )

    loads = [
        pltpu.make_async_copy(out_s, weights.at[s, OUT_S:QKV_T, :], load_sem.at[0]),
        pltpu.make_async_copy(qkv_t, weights.at[s, QKV_T:OUT_T, :], load_sem.at[1]),
        pltpu.make_async_copy(out_t, weights.at[s, OUT_T : OUT_T + 144, :], load_sem.at[2]),
        pltpu.make_async_copy(qkv_s_in, qkv_s, load_sem.at[3]),
        pltpu.make_async_copy(table_in, table, load_sem.at[4]),
    ]
    for load in loads:
        load.start()
    for j in range(2):
        lat_send[j] = latents[j].astype(BF)
    weights[s, OUT_T + 144 :, :] = jnp.zeros((SHARD - OUT_T - 144, D), BF)
    half = iota((8, 128), 0) < SUB
    own_steps = jnp.where(half, steps[0], steps[1]).astype(F32)
    step_rows[pl.ds(pl.multiple_of(f * 8, 8), 8), :] = own_steps
    step_rows[ROWS:, :] = jnp.zeros((8, 128), F32)
    vel_send[NF:] = jnp.zeros((1, 1, 128), F32)

    pl.semaphore_wait(barrier, NF + NS - 1)

    def lat_copy(k):
        return push(lat_send, lat_all.at[s], lat_ssem.at[k], lat_rsem.at[s], (f, space_peer(k)))

    def lat_wait(k):
        origin = space_peer(k)
        push(lat_send, lat_all.at[origin], lat_ssem.at[k], lat_rsem.at[origin], (f, origin)).wait_recv()

    def next_copy():
        return push(latents.at[0], lat_next, next_sem.at[0], next_sem.at[1], (frame_peer(NF - 1), s))

    def step_copy(k, row):
        rows = pl.ds(pl.multiple_of(row * 8, 8), 8)
        return push(
            step_rows.at[rows], step_rows.at[rows], step_ssem.at[k], step_rsem.at[row], (frame_peer(k), s)
        )

    @pl.loop(1, NS)
    def _(k):
        lat_copy(k).start()

    own_lat = pltpu.make_async_copy(lat_send, lat_all.at[s], own_sem.at[0])
    own_lat.start()

    def quarter(m):
        return lax.rem(yl + m // 2, 2) * 2 + lax.rem(z + m % 2, 2)

    def near(j, who):
        turn = 1 - 2 * who
        return (x, lax.rem(x - turn + 4, 4), lax.rem(x + turn + 4, 4), lax.rem(x + 2, 4))[j]

    def block(i, who):
        j = i % 4
        if i < 4:
            return near(1, who) * 2 + yh, quarter(j) * 2, 2
        if i < 8:
            return near(3, who) * 2 + yh, quarter(j) * 2 + who, 1
        return near(j, who) * 2 + 1 - yh, quarter((2, 0, 3, 1)[i // 4 - 2]) * 2 + who, 1

    def hop_source(i):
        if i < 4:
            return s, quarter(i) * 2, 2
        if i < 8:
            share, part, _ = block(i - 4, c)
            return share, part + c, 1
        if i < 12:
            return near(i - 8, c) * 2 + yh, quarter(0) * 2 + c, 1
        return block(i - 4 if i < 16 else i - 8, c)

    def place(share, part, count):
        return weights.at[share, pl.ds(pl.multiple_of(part * PART, PART), PART * count), :]

    def hop(i, spot):
        target = to_x if i < 8 else to_cross if i < 12 else to_side if i < 16 else to_z
        return push(spot, spot, dir_ssem.at[i], dir_rsem.at[i], target)

    def hop_start(i):
        hop(i, place(*hop_source(i))).start()

    def core_copy(i, who):
        spot = place(*block(i, who))
        return push(spot, spot, core_ssem.at[i], core_rsem.at[i], to_core)

    then = {0: (9, 4, 2), 1: (5, 3), 2: (6,), 3: (7,), 4: (11,)}
    for j in range(4):
        then[8 + j] = (16 + j, 12 + j)
        then[12 + j] = (20 + j,)

    def take(*hops):
        for i in hops:
            if i is None:
                core_copy(0, 1 - c).wait_recv()
                hop_start(10)
                continue
            hop(i, place(*block(i, c))).wait_recv()
            core_copy(i, c).start()
            for k in then.get(i, ()):
                hop_start(k)

    for load in loads[:3]:
        load.wait()
    hop_start(0)
    hop_start(8)
    hop_start(1)

    @pl.loop(1, NF)
    def _(k):
        step_copy(k, f).start()

    next_copy().start()

    base = embed[...].astype(F32)
    center = base - jnp.mean(base, axis=1, keepdims=True)
    gram = dot(center, center, NT, lax.Precision.HIGHEST) * (1.0 / D)
    gram3 = jnp.concatenate(split3(gram), axis=1)
    eye = (iota((HD, HD), 0) == iota((HD, HD), 1)).astype(F32)
    gains_s = dot(eye, gain_s[...], NT, lax.Precision.HIGHEST)
    gains_t = dot(eye, gain_t[...], NT, lax.Precision.HIGHEST)
    loads[4].wait()
    slot = iota((16, 8 * STEPS), 1) - iota((16, 8 * STEPS), 0) % 8
    wanted = jnp.where(iota((16, 8 * STEPS), 0) < 8, steps[0], steps[1]) * 8
    both_mods = dot((slot == wanted).astype(BF), table[...])
    own_mods = [both_mods[:8], both_mods[8:]]
    parts = []
    for j in range(2):
        parts.extend(split2(center * (1.0 + own_mods[j][1:2, :])))
    parts.append(jnp.concatenate(own_mods, axis=0).astype(BF))
    stack = jnp.concatenate(parts, axis=0)
    loads[3].wait()
    mixed = dot(qkv_s[...], stack, NT)

    own_lat.wait()

    @pl.loop(1, NS)
    def _(k):
        lat_wait(k)

    def project_frame(j):
        lat = jnp.concatenate([lat_all[i, j] for i in range(NS)], axis=1)
        lat32 = lat.astype(F32)
        spread = jnp.sum(lat32 * dot(gram3, jnp.concatenate([lat] * 3, axis=0)), axis=0, keepdims=True)
        rstd = lax.rsqrt(jnp.maximum(spread, 0.0) + EPS)
        matrix = mixed[:, 32 * j : 32 * j + 16] + mixed[:, 32 * j + 16 : 32 * j + 32]
        shift = mixed[:, 64 + 8 * j : 65 + 8 * j]
        matrix2 = jnp.concatenate(split2(matrix), axis=1)
        projected = dot(matrix2, jnp.concatenate([lat] * 2, axis=0)) * rstd + shift
        ones = (iota((8, TOK), 0) == 0).astype(F32)
        for h in range(2):
            at = h * 3 * HD
            query = head_norm(projected[at : at + HD], gains_s[:, 0:1]) * SCORE
            keys = head_norm(projected[at + HD : at + 2 * HD], gains_s[:, 1:2])
            values = projected[at + 2 * HD : at + 3 * HD]
            qb[h] = query.astype(BF)
            kb[h] = keys.T.astype(BF)
            vb[h] = jnp.concatenate([values, ones], axis=0).astype(BF)

    def attend_head(h):
        chunk = 512

        @pl.loop(0, TOK // chunk)
        def _(i):
            columns = pl.ds(pl.multiple_of(i * chunk, chunk), chunk)
            scores = dot(kb[h], qb[h, :, columns])
            weighted = dot(vb[h], jnp.exp2(scores).astype(BF))
            att_f[h * HD : (h + 1) * HD, columns] = weighted[:HD] / weighted[HD : HD + 1]

    def share_rows(share):
        return pl.ds(pl.multiple_of(share * 144, 16), 144)

    def share_columns(share):
        return pl.ds(pl.multiple_of(share * OWN, OWN), OWN)

    def att_copy(j, k):
        peer = space_peer(k)
        return push(
            att.at[j, :, share_columns(peer)], att_in.at[j, share_rows(s), :],
            att_ssem.at[j, k], att_rsem.at[j, s], (f, peer),
        )

    def att_wait(j, k):
        origin = space_peer(k)
        push(
            att.at[j, :, share_columns(origin)], att_in.at[j, share_rows(origin), :],
            att_ssem.at[j, k], att_rsem.at[j, origin], (f, origin),
        ).wait_recv()

    def att_own(j):
        return pltpu.make_async_copy(
            att.at[j, :, share_columns(s)], att_in.at[j, share_rows(s), :], own_sem.at[1 + j]
        )

    stops = iter(((0, 8, None), (1, 16), (12, 9, 4), (17, 20), (10, 2), (13, 5, 11), (18, 14), (3, 21), (19, 6, 15, 22), (7, 23)))
    for j in range(2):
        take(*next(stops))
        project_frame(j)
        take(*next(stops))
        attend_head(0)
        take(*next(stops))
        attend_head(1)
        att[j] = att_f[...].astype(BF)

        @pl.loop(1, NS)
        def _(k):
            att_copy(j, k).start()

        att_own(j).start()

    take(*next(stops))

    for j in range(2):
        att_own(j).wait()

        @pl.loop(1, NS)
        def _(k):
            att_wait(j, k)

    take(*next(stops))

    row, column = iota((16 * NF, 2 * OWN), 0), iota((16 * NF, 2 * OWN), 1)
    matching = column == row % 8 // SUB * OWN + row // 16 * SUB + row % SUB
    upper = row // 8 % 2 == 0
    own_lats = jnp.concatenate([lat_send[0], lat_send[1]], axis=1)
    tail = jnp.concatenate([own_lats, jnp.zeros((WIDE - D // 2 - PATCH, 2 * OWN), BF)], axis=0)
    both = jnp.concatenate([att_in[0], att_in[1]], axis=1)
    gathered = jnp.zeros((16 * NF, WIDE), F32)
    for h in range(2):
        piece = jnp.concatenate([both[h * (D // 2) : (h + 1) * (D // 2)], tail], axis=0)
        gathered += dot((matching & (upper == (h == 0))).astype(BF), piece, NT)
    send[...] = gathered.astype(BF)

    def row_copy(k):
        peer = frame_peer(k)
        return push(
            send.at[pl.ds(pl.multiple_of(peer * 16, 16), 16), :],
            recv.at[pl.ds(pl.multiple_of(f * 16, 16), 16), :],
            row_ssem.at[k], row_rsem.at[f], (peer, s),
        )

    def row_wait(k):
        origin = frame_peer(k)
        rows = pl.ds(pl.multiple_of(origin * 16, 16), 16)
        push(send.at[rows, :], recv.at[rows, :], row_ssem.at[k], row_rsem.at[origin], (origin, s)).wait_recv()

    @pl.loop(1, NF)
    def _(k):
        row_copy(k).start()

    own_rows = pl.ds(pl.multiple_of(f * 16, 16), 16)
    own_copy = pltpu.make_async_copy(send.at[own_rows, :], recv.at[own_rows, :], own_sem.at[3])
    own_copy.start()

    take(*next(stops))

    @pl.loop(1, NF)
    def _(k):
        step_copy(k, frame_peer(k)).wait_recv()

    wanted = jnp.concatenate([step_rows[0:ROWS, :]] * 8, axis=1) * 8.0
    slots = iota((ROWS, 8 * STEPS), 1).astype(F32)
    for kind in range(6):
        mods[kind] = dot((wanted + (kind + 2.0) == slots).astype(BF), table[...])

    take(*next(stops))
    own_copy.wait()

    @pl.loop(1, NF)
    def _(k):
        row_wait(k)

    row, column = iota((ROWS, 16 * NF), 0), iota((ROWS, 16 * NF), 1)
    halves = [
        dot((column == row // 8 * 16 + h * 8 + row % 8).astype(BF), recv[...]) for h in range(2)
    ]
    hidden = dot(halves[0][:, D // 2 : D // 2 + PATCH].astype(BF), embed[...])
    for i in range(1, HOPS):
        core_copy(i, 1 - c).wait_recv()

    output = jnp.zeros((ROWS, D), F32)
    for i in range(NS):
        at = i % 4 * 144
        output += dot(halves[i // 4][:, at : at + 144].astype(BF), weights[i, OUT_S:QKV_T, :])
    hidden += mods[0] * output

    ready = (layer_norm(hidden) * (1.0 + mods[2]) + mods[1]).astype(BF)
    for i in range(NS):
        proj[i] = dot(weights[i, QKV_T:OUT_T, :], ready, NT)
    same = iota((ROWS, ROWS), 0) % SUB == iota((ROWS, ROWS), 1) % SUB
    ones = (iota((8, ROWS), 0) == 0).astype(F32)

    @pl.loop(0, NS // 2)
    def _(i):
        for n in range(4):
            share, at = 2 * i + n // 2, n % 2 * 3 * HD
            query = head_norm(proj[share, at : at + HD, :], gains_t[:, 0:1]) * SCORE
            keys = head_norm(proj[share, at + HD : at + 2 * HD, :], gains_t[:, 1:2])
            values = jnp.concatenate([proj[share, at + 2 * HD : at + 3 * HD, :], ones], axis=0).astype(BF)
            scores = dot(keys.T.astype(BF), query.astype(BF))
            weighted = dot(values, jnp.where(same, jnp.exp2(scores), 0.0).astype(BF))
            rows = pl.ds(pl.multiple_of((4 * i + n) * HD, 8), HD)
            att_t[rows, :] = weighted[:HD] / weighted[HD : HD + 1]

    output = jnp.zeros((ROWS, D), F32)
    for i in range(NS):
        output += dot(att_t[144 * i : 144 * i + 144, :].T.astype(BF), weights[i, OUT_T : OUT_T + 144, :])
    hidden += mods[3] * output
    ready = (layer_norm(hidden) * (1.0 + mods[5]) + mods[4]).astype(BF)
    wide = dot(ready, jnp.concatenate([final[...]] * 8, axis=0), NT)
    wide = jnp.where(iota((ROWS, 128), 0) % 8 == iota((ROWS, 128), 1) // PATCH, wide, 0.0)
    vel_send[0:NF] = jnp.sum(wide.reshape(NF, 8, 128), axis=1, keepdims=True)

    def vel_copy(k):
        peer = frame_peer(k)
        return push(
            vel_send.at[pl.ds(peer, 2)], vel_recv.at[f],
            vel_ssem.at[k], vel_rsem.at[f], (peer, s),
        )

    def vel_wait(k):
        origin = frame_peer(k)
        push(
            vel_send.at[pl.ds(origin, 2)], vel_recv.at[origin],
            vel_ssem.at[k], vel_rsem.at[origin], (origin, s),
        ).wait_recv()

    @pl.loop(1, NF)
    def _(k):
        vel_copy(k).start()

    own_vel = pltpu.make_async_copy(
        vel_send.at[pl.ds(f, 2)], vel_recv.at[f], own_sem.at[4]
    )
    own_vel.start()
    next_copy().wait_recv()
    own_vel.wait()

    @pl.loop(1, NF)
    def _(k):
        vel_wait(k)

    turned = [vel_recv[:, i, 0, :].T for i in range(2)]
    row, column = iota((NF, OWN), 0), iota((NF, OWN), 1)
    updated = []
    for j in range(3):
        found = jnp.zeros((PATCH, OWN), F32)
        for t in range(SUB):
            at = (j % 2 * SUB + t) * PATCH
            mine = jnp.concatenate(split3(turned[j // 2][at : at + PATCH]), axis=0)
            spread = dot(mine, (column == SUB * row + t).astype(BF))
            found += spread[0:16] + spread[16:32] + spread[32:48]
        index = step_rows[pl.ds(f * 8 + j * SUB, 1), :]
        size = level(index + 1.0) - level(index)
        if j < 2:
            result[j] = found
        updated.append((latents[j] if j < 2 else lat_next[...]) - size * found)
    result[2] = updated[1]
    result[3] = jnp.where(f == NF - 1, noise[...], updated[2])

    for j in range(2):

        @pl.loop(1, NS)
        def _(k):
            att_copy(j, k).wait_send()

    @pl.loop(1, NS)
    def _(k):
        lat_copy(k).wait_send()

    @pl.loop(1, NF)
    def _(k):
        step_copy(k, f).wait_send()
        row_copy(k).wait_send()
        vel_copy(k).wait_send()

    next_copy().wait_send()
    for i in range(HOPS):
        hop(i, place(*hop_source(i))).wait_send()
        core_copy(i, c).wait_send()


def local(
    latents, time_index, fresh_noise, modulation_table, embed_weight, spatial_qkv, spatial_out,
    temporal_qkv, temporal_out, final_weight, spatial_gain, temporal_gain,
):
    dma = pltpu.SemaphoreType.DMA
    vmem = pl.BlockSpec(memory_space=pltpu.VMEM)
    hbm = pl.BlockSpec(memory_space=pl.ANY)
    smem = pl.BlockSpec(memory_space=pltpu.SMEM)
    result = pl.pallas_call(
        kernel,
        out_shape=jax.ShapeDtypeStruct((4, PATCH, OWN), F32),
        in_specs=[vmem, smem, vmem, hbm, vmem, hbm, hbm, hbm, hbm, vmem, vmem, vmem],
        out_specs=vmem,
        scratch_shapes=[
            pltpu.VMEM((8 * STEPS, D), BF),
            pltpu.VMEM((432, D), BF),
            pltpu.VMEM((NS, SHARD, D), BF),
            pltpu.VMEM((2, PATCH, OWN), BF),
            pltpu.VMEM((NS, 2, PATCH, OWN), BF),
            pltpu.VMEM((PATCH, OWN), F32),
            pltpu.VMEM((ROWS + 8, 128), F32),
            pltpu.VMEM((2, HD, TOK), BF),
            pltpu.VMEM((2, TOK, HD), BF),
            pltpu.VMEM((2, HD + 8, TOK), BF),
            pltpu.VMEM((144, TOK), F32),
            pltpu.VMEM((2, 144, TOK), BF),
            pltpu.VMEM((2, D, OWN), BF),
            pltpu.VMEM((16 * NF, WIDE), BF),
            pltpu.VMEM((16 * NF, WIDE), BF),
            pltpu.VMEM((6, ROWS, D), F32),
            pltpu.VMEM((NS, 432, ROWS), F32),
            pltpu.VMEM((D, ROWS), F32),
            pltpu.VMEM((NF + 1, 1, 128), F32),
            pltpu.VMEM((NF, 2, 1, 128), F32),
            dma((NS,)),
            dma((NS,)),
            dma((2,)),
            dma((NF,)),
            dma((NF,)),
            dma((HOPS,)),
            dma((HOPS,)),
            dma((HOPS,)),
            dma((HOPS,)),
            dma((2, NS)),
            dma((2, NS)),
            dma((NF,)),
            dma((NF,)),
            dma((NF,)),
            dma((NF,)),
            dma((5,)),
            dma((5,)),
        ],
        compiler_params=pltpu.CompilerParams(
            collective_id=0, has_side_effects=True, vmem_limit_bytes=60 * 1024 * 1024
        ),
    )(
        latents, time_index, fresh_noise, modulation_table.reshape(STEPS * 8, D), embed_weight,
        spatial_qkv.T, spatial_out, temporal_qkv.T, temporal_out, final_weight.T, spatial_gain, temporal_gain,
    )
    return result[:2], result[2:]


def solution(mesh):
    return jax.shard_map(
        local,
        mesh=mesh,
        in_specs=(
            P("frame", None, "space"),
            P("frame"),
            P(None, "space"),
            P(),
            P(),
            P(None, "space"),
            P("space", None),
            P(None, "space"),
            P("space", None),
            P(),
            P(),
            P(),
        ),
        out_specs=(P("frame", None, "space"), P("frame", None, "space")),
        check_vma=False,
    )
```
